128 devices in a mesh: segment: 16 (over y, z_hi, core), rows: 8 (over x, z_lo).
Axes of the slice: x: 4, y: 4, z: 4 (z_hi: 2, z_lo: 2; z = z_hi * 2 + z_lo), core: 2. Of those that a mesh axis runs over, the one named last changes fastest.
Arguments:
- held_maps: bfloat16 [16, 128, 64, 256], P('segment', 'rows'), may hold values from -6 to 6
- held_skips: bfloat16 [3, 16, 128, 64, 256], P(None, 'segment', 'rows'), may hold values from -6 to 6
- arrivals: bfloat16 [3, 128, 64, 256], P(None, 'rows'), may hold values from -6 to 6
- kernels: bfloat16 [16, 3, 3, 768, 256], P('segment'), may hold values from -0.125 to 0.125
- biases: float32 [16, 3, 256], P('segment'), may hold values from -3 to 3
Outputs:
- section_maps: bfloat16 [3, 16, 128, 64, 256], P(None, 'segment', 'rows')
- skip_stash: bfloat16 [3, 16, 128, 64, 256], P(None, 'segment', 'rows')
The draws below stay inside these ranges and needn't reach their ends.
All inputs are finite; a program needn't handle non-finite values.
Results may differ from the reference program's by a relative error of at most 0.0075.
Values may be sent and summed in bfloat16 or wider, within the bound.
No kernel may reach another device: no remote copies, remote signals or barrier semaphores. Data moves between devices by JAX's collectives and lax.ppermute only.
A program may use at most 64 MiB of HBM per device.

```python
import jax
import jax.numpy as jnp
from jax import lax

C = 256
W = 64
TICKS = 3
CONVS = 3
H = 128
N_SEGMENT = 16


def shard_levels(stream_key, dims, shards, least, top_value):
    level, own = 1.0, jax.random.fold_in(stream_key, 6)
    for dim, parts in shards:
        draws = jnp.exp(jax.random.uniform(jax.random.fold_in(own, dim), (parts,), jnp.float32, least / len(shards), top_value / len(shards)))
        level = level * jnp.repeat(draws, dims[dim] // parts).reshape([-1 if axis == dim else 1 for axis in range(len(dims))])
    return level


def gaussian(own_key, shape, width, bound, shards=(), held_as=jnp.bfloat16):
    values = width * jax.random.normal(own_key, shape, jnp.float32)
    if shards:
        values = values * shard_levels(own_key, shape, shards, -0.22, 0.18)
    return jnp.clip(values, -bound, bound).astype(held_as)


def setup_inputs(seed: int = 0) -> dict:
    arg_keys = jax.random.split(jax.random.key(seed), 6)
    held_maps = gaussian(arg_keys[0], (N_SEGMENT, H, W, C), 1.0, 6.0, ((0, 16), (1, 8)))
    held_skips = gaussian(arg_keys[1], (TICKS, N_SEGMENT, H, W, C), 1.0, 6.0, ((1, 16), (2, 8)))
    arrivals = gaussian(arg_keys[2], (TICKS, H, W, C), 1.0, 6.0, ((1, 8),))
    kernels = gaussian(arg_keys[3], (N_SEGMENT, CONVS, 3, 3 * C, C), (9 * C) ** -0.5, 0.125, ((0, 16),))
    biases = gaussian(arg_keys[4], (N_SEGMENT, CONVS, C), 0.5, 3.0, ((0, 16),), jnp.float32)
    return {"held_maps": held_maps, "held_skips": held_skips, "arrivals": arrivals, "kernels": kernels, "biases": biases}


def convolve(source, kernel, offsets):
    rows_out = source.shape[0] - 2
    columns_count = source.shape[1]
    padded = jnp.pad(source, ((0, 0), (1, 1), (0, 0)))
    columns = jnp.concatenate([padded[:, 0:columns_count], padded[:, 1:columns_count + 1], padded[:, 2:columns_count + 2]], axis=-1)
    summed = jnp.zeros((rows_out * columns_count, kernel.shape[2]), jnp.float32)
    for row_offset in range(3):
        block = columns[row_offset:row_offset + rows_out].reshape(rows_out * columns_count, -1)
        summed = summed + jnp.dot(block, kernel[row_offset], preferred_element_type=jnp.float32)
    return summed.reshape(rows_out, columns_count, -1) + offsets


def pad_rows(source):
    return jnp.pad(source, ((1, 1), (0, 0), (0, 0)))


def run_section(operands):
    section_in, kernel, offsets = operands
    hidden_state = section_in
    for layer_index in range(2):
        hidden_state = jax.nn.silu(convolve(pad_rows(hidden_state), kernel[layer_index], offsets[layer_index])).astype(jnp.bfloat16)
    summed = section_in.astype(jnp.float32) + convolve(pad_rows(hidden_state), kernel[2], offsets[2])
    return summed.astype(jnp.bfloat16)


def reference(held_maps, held_skips, arrivals, kernels, biases):
    previous = held_maps
    half = N_SEGMENT // 2
    section_results = []
    stored_skips = []
    for tick in range(TICKS):
        incoming = jnp.concatenate([arrivals[tick][None], previous[:-1]], axis=0)
        joined = []
        for section in range(N_SEGMENT):
            if section < half:
                joined.append(incoming[section])
            else:
                delay = 2 * section - N_SEGMENT + 1
                if tick >= delay:
                    skip = section_results[tick - delay][N_SEGMENT - 1 - section]
                else:
                    skip = held_skips[tick, section]
                joined.append((incoming[section].astype(jnp.float32) + skip.astype(jnp.float32)).astype(jnp.bfloat16))
        section_in = jnp.stack(joined)
        new_activation = lax.map(run_section, (section_in, kernels, biases))
        section_results.append(new_activation)
        decoder_marker = (jnp.arange(N_SEGMENT) >= half)[:, None, None, None]
        stored_skips.append(jnp.where(decoder_marker, new_activation[::-1], jnp.zeros_like(new_activation)))
        previous = new_activation
    return jnp.stack(section_results), jnp.stack(stored_skips)
```

```python
import functools

import jax
import jax.numpy as jnp
from jax import lax
from jax.experimental import pallas as pl
from jax.experimental.pallas import tpu as pltpu
from jax.sharding import PartitionSpec as P

TICKS = 3
SECTIONS = 16
RANKS = 8
ROWS = 16
W = 64
C = 256
AXES = ("segment", "rows")
VMEM_LIMIT = 26 * 2**20


def tiles(total, size):
    return [(start, min(size, total - start)) for start in range(0, total, size)]


def put(dst, row, count, value):
    column = lax.broadcasted_iota(jnp.int32, value.shape, 0) % W
    left = jnp.where(column == 0, 0.0, pltpu.roll(value, 1, 0))
    right = jnp.where(column == W - 1, 0.0, pltpu.roll(value, value.shape[0] - 1, 0))
    rows = pl.ds(row * W, count * W)
    dst[rows, 0:C] = left.astype(jnp.bfloat16)
    dst[rows, C : 2 * C] = value.astype(jnp.bfloat16)
    dst[rows, 2 * C : 3 * C] = right.astype(jnp.bfloat16)


def conv(src, row, count, kernel_ref, bias_ref, layer):
    lhs = jnp.concatenate(
        [src[pl.ds((row + d) * W, count * W), :] for d in range(3)], axis=1
    )
    weights = kernel_ref[layer].reshape(9 * C, C)
    return jnp.dot(lhs, weights, preferred_element_type=jnp.float32) + bias_ref[layer : layer + 1]


def silu(v):
    return v * (0.5 * jnp.tanh(0.5 * v) + 0.5)


def section_kernel(
    tick, core, grow, pieces, n_order,
    place_ref, skips_ref, arrivals_ref, aux_up_ref, aux_down_ref, kernel_ref, bias_ref, *rest,
):
    inc_refs = rest[: len(pieces)]
    out_ref = rest[len(pieces) + n_order]
    aux_ref, x_ref, a_ref, b_ref, aux_sem = rest[len(pieces) + n_order + 1 :]
    segment, rank = place_ref[0], place_ref[1]
    halo = grow + 3
    total = ROWS + 2 * halo

    @pl.when(lax.rem(segment, 2) == core)
    def _():
        first = segment == 0
        decoder = segment >= SECTIONS // 2
        with_aux = jnp.logical_or(first, decoder)
        load_arrival = pltpu.make_async_copy(arrivals_ref.at[tick], aux_ref, aux_sem)
        load_skip = pltpu.make_async_copy(skips_ref.at[tick, 0], aux_ref, aux_sem)

        @pl.when(first)
        def _():
            load_arrival.start()
            load_arrival.wait()

        @pl.when(decoder)
        def _():
            load_skip.start()
            load_skip.wait()

        n_up = aux_up_ref.shape[1]

        def aux_rows(row, count):
            if row < halo:
                return aux_up_ref[0, pl.ds(n_up - halo + row, count)]
            if row < halo + ROWS:
                return aux_ref[pl.ds(row - halo, count)]
            return aux_down_ref[0, pl.ds(row - halo - ROWS, count)]

        def fill(add_aux):
            for index, (start, low, length) in enumerate(pieces):
                cuts = sorted(
                    {start, start + length}
                    | {c for c in (halo, halo + ROWS) if start < c < start + length}
                )
                for begin, end in zip(cuts, cuts[1:]):
                    for offset, count in tiles(end - begin, 2):
                        row = begin + offset
                        value = inc_refs[index][pl.ds(low + row - start, count)].astype(jnp.float32)
                        if add_aux:
                            other = aux_rows(row, count).astype(jnp.float32)
                            if tick >= 1:
                                other = jnp.where(segment == SECTIONS // 2, value, other)
                            value = value + other
                        value = value.reshape(count * W, C)
                        x_ref[pl.ds(row * W, count * W)] = value.astype(jnp.bfloat16)
                        put(a_ref, row, count, value)

        @pl.when(with_aux)
        def _():
            fill(True)

        @pl.when(jnp.logical_not(with_aux))
        def _():
            fill(False)

        def inside(value, row, count, reach):
            if row >= reach and row + count <= reach + ROWS:
                return value
            line = row - reach + lax.broadcasted_iota(jnp.int32, value.shape, 0) // W
            outside = jnp.logical_or(
                jnp.logical_and(rank == 0, line < 0),
                jnp.logical_and(rank == RANKS - 1, line >= ROWS),
            )
            return jnp.where(outside, 0.0, value)

        for row, count in tiles(total - 2, 4):
            value = silu(conv(a_ref, row, count, kernel_ref, bias_ref, 0))
            put(b_ref, row, count, inside(value, row, count, halo - 1))
        for row, count in tiles(total - 4, 4):
            value = silu(conv(b_ref, row, count, kernel_ref, bias_ref, 1))
            put(a_ref, row, count, inside(value, row, count, halo - 2))
        for row, count in tiles(total - 6, 4):
            value = conv(a_ref, row, count, kernel_ref, bias_ref, 2)
            value = value + x_ref[pl.ds((row + 3) * W, count * W)].astype(jnp.float32)
            value = inside(value, row, count, halo - 3)
            out_ref[pl.ds(row, count)] = value.astype(jnp.bfloat16).reshape(count, W, C)


def section(name, tick, core, grow, place, skips, arrivals, aux, weights, biases, incoming, order):
    halo = grow + 3
    total = ROWS + 2 * halo
    rows = 54 + 6 * grow
    vmem = pl.BlockSpec(memory_space=pltpu.VMEM)
    anywhere = pl.BlockSpec(memory_space=pl.ANY)
    return pl.pallas_call(
        functools.partial(
            section_kernel, tick, core, grow, tuple(p[1:] for p in incoming), len(order)
        ),
        out_shape=jax.ShapeDtypeStruct((ROWS + 2 * grow, W, C), jnp.bfloat16),
        in_specs=[pl.BlockSpec(memory_space=pltpu.SMEM), anywhere, anywhere]
        + [vmem] * (4 + len(incoming))
        + [anywhere] * len(order),
        out_specs=vmem,
        scratch_shapes=[
            pltpu.VMEM((ROWS, W, C), jnp.bfloat16),
            pltpu.VMEM((total * W, C), jnp.bfloat16),
            pltpu.VMEM((total * W, 3 * C), jnp.bfloat16),
            pltpu.VMEM(((total - 2) * W, 3 * C), jnp.bfloat16),
            pltpu.SemaphoreType.DMA,
        ],
        compiler_params=pltpu.CompilerParams(vmem_limit_bytes=VMEM_LIMIT),
        cost_estimate=pl.CostEstimate(
            flops=rows * W * 9 * C * C * 2, bytes_accessed=4 * 2**20, transcendentals=0
        ),
        name=name,
    )(
        place, skips, arrivals, *aux, weights, biases, *[p[0] for p in incoming], *order
    )


def move(x, pairs):
    return lax.ppermute(x, AXES, pairs)


def links(step, sources, by=0):
    return [
        (s * RANKS + r, step(s) * RANKS + r + by)
        for s in sources
        for r in range(RANKS)
        if 0 <= r + by < RANKS
    ]


def following(s):
    return s + 1


def same(s):
    return s


def mirror(s):
    return SECTIONS - 1 - s


EVEN = range(0, SECTIONS - 1, 2)
ODD = range(1, SECTIONS - 1, 2)
ALL = range(SECTIONS - 1)
AUX = [0] + list(range(SECTIONS // 2, SECTIONS))
HALF = SECTIONS // 2


def on_device(held_maps, held_skips, arrivals, kernels, biases):
    segment = lax.axis_index("segment")
    rank = lax.axis_index("rows")
    place = jnp.stack([segment, rank]).astype(jnp.int32)
    even = lax.rem(segment, 2) == 0
    weights, bias = kernels[0], biases[0]
    held = held_maps[0]

    def aux_edges(ticks, count):
        first = segment == 0
        low = jnp.where(first, arrivals[ticks, :count], held_skips[ticks, 0, :count])
        high = jnp.where(first, arrivals[ticks, ROWS - count :], held_skips[ticks, 0, ROWS - count :])
        return (
            move(high, links(same, AUX, 1)),
            move(low, links(same, AUX, -1)),
        )

    def part(name, tick, core, grow, aux, incoming, order=()):
        return section(
            name, tick, core, grow, place, held_skips, arrivals, aux, weights, bias, incoming, order
        )

    def split(main, up, down, grow):
        halo = grow + 3
        have = up.shape[0]
        return [
            (up, 0, have - halo, halo),
            (main, halo, 0, ROWS),
            (down, halo + ROWS, 0, halo),
        ]

    off0 = move(held, links(following, ODD))
    up0 = move(held[ROWS - 6 :], links(following, ALL, 1))
    down0 = move(held[:6], links(following, ALL, -1))
    on0 = move(held, links(following, EVEN))
    aux0 = aux_edges(slice(0, 1), 6)
    b0 = part("b0", 0, 1, 0, aux0, split(on0, up0, down0, 0))

    off1 = move(b0, links(following, ODD))
    up1 = move(b0[ROWS - 6 :], links(following, ODD, 1))
    down1 = move(b0[:6], links(following, ODD, -1))
    aux1 = aux_edges(slice(1, 2), 6)
    aux2 = aux_edges(slice(2, 3), 3)
    stash0b = move(b0, links(mirror, range(1, HALF, 2)))
    a0 = part("a0", 0, 0, 3, aux0, split(off0, up0, down0, 3), (b0,))

    on1 = move(a0, links(following, EVEN))
    stash0a = move(a0[3:19], links(mirror, range(0, HALF, 2)))
    b1 = part("b1", 1, 1, 0, aux1, [(on1, 0, 0, 22)])

    off2 = move(b1, links(following, ODD))
    up2 = move(b1[ROWS - 3 :], links(following, ODD, 1))
    down2 = move(b1[:3], links(following, ODD, -1))
    stash1b = move(b1, links(mirror, range(1, HALF, 2)))
    a1 = part("a1", 1, 0, 3, aux1, split(off1, up1, down1, 3), (b1,))

    on2 = move(a1, links(following, EVEN))
    stash1a = move(a1[3:19], links(mirror, range(0, HALF, 2)))
    b2 = part("b2", 2, 1, 0, aux2, [(on2, 0, 0, 22)])
    stash2b = move(b2, links(mirror, range(1, HALF, 2)))
    a2 = part("a2", 2, 0, 0, aux2, split(off2, up2, down2, 0), (b2,))
    stash2a = move(a2, links(mirror, range(0, HALF, 2)))

    maps = jnp.stack(
        [
            jnp.where(even, a0[3:19], b0),
            jnp.where(even, a1[3:19], b1),
            jnp.where(even, a2, b2),
        ]
    )
    stash = jnp.stack(
        [
            jnp.where(even, stash0b, stash0a),
            jnp.where(even, stash1b, stash1a),
            jnp.where(even, stash2b, stash2a),
        ]
    )
    return maps[:, None], stash[:, None]


def solution(mesh):
    placed = (
        P("segment", "rows", None, None),
        P(None, "segment", "rows", None, None),
        P(None, "rows", None, None),
        P("segment", None, None, None, None),
        P("segment", None, None),
    )
    out = P(None, "segment", "rows", None, None)
    return jax.shard_map(
        on_device, mesh=mesh, in_specs=placed, out_specs=(out, out), check_vma=False
    )
```

```python
import functools

import jax
import jax.numpy as jnp
from jax import lax
from jax.experimental import pallas as pl
from jax.experimental.pallas import tpu as pltpu
from jax.sharding import PartitionSpec as P

TICKS = 3
SECTIONS = 16
RANKS = 8
HALO = 3
ROWS = 16
W = 64
C = 256
AXES = ("segment", "rows")
VMEM_LIMIT = 26 * 2**20


def tiles(total, size):
    return [(start, min(size, total - start)) for start in range(0, total, size)]


def put(dst, row, count, value):
    column = lax.broadcasted_iota(jnp.int32, value.shape, 0) % W
    left = jnp.where(column == 0, 0.0, pltpu.roll(value, 1, 0))
    right = jnp.where(column == W - 1, 0.0, pltpu.roll(value, value.shape[0] - 1, 0))
    rows = pl.ds(row * W, count * W)
    dst[rows, 0:C] = left.astype(jnp.bfloat16)
    dst[rows, C : 2 * C] = value.astype(jnp.bfloat16)
    dst[rows, 2 * C : 3 * C] = right.astype(jnp.bfloat16)


def conv(src, row, count, weights, bias_ref, layer):
    lhs = jnp.concatenate(
        [src[pl.ds((row + d) * W, count * W), :] for d in range(3)], axis=1
    )
    return (
        jnp.dot(lhs, weights[layer].reshape(9 * C, C), preferred_element_type=jnp.float32)
        + bias_ref[layer : layer + 1]
    )


def silu(v):
    return v * (0.5 * jnp.tanh(0.5 * v) + 0.5)


def section_kernel(
    tick, n_order,
    skips_ref, arrivals_ref, kernel_ref, bias_ref, aux_up_ref, aux_down_ref,
    main_ref, up_ref, down_ref, *rest,
):
    out_ref, aux_ref, x_ref, a_ref, b_ref, aux_sem = rest[n_order:]
    segment, rank = lax.axis_index("segment"), lax.axis_index("rows")
    total = ROWS + 2 * HALO
    first = segment == 0
    decoder = segment >= SECTIONS // 2
    load_arrival = pltpu.make_async_copy(arrivals_ref.at[tick], aux_ref, aux_sem)
    load_skip = pltpu.make_async_copy(skips_ref.at[tick, 0], aux_ref, aux_sem)

    @pl.when(first)
    def _():
        load_arrival.start()

    @pl.when(decoder)
    def _():
        load_skip.start()

    def fill(role):
        pieces = ((0, HALO, up_ref, aux_up_ref), (HALO + ROWS, HALO, down_ref, aux_down_ref),
                  (HALO, ROWS, main_ref, None))
        for low, length, source, aux in pieces:
            if aux is None and role == "first":
                source = aux_ref
            for offset, count in tiles(length, 2):
                rows = pl.ds(offset, count)
                value = source[rows].astype(jnp.float32)
                if role == "decoder":
                    if aux is None:
                        other = aux_ref[rows]
                    else:
                        other = aux[tick, rows]
                    other = other.astype(jnp.float32)
                    if tick >= 1:
                        other = jnp.where(segment == SECTIONS // 2, value, other)
                    value = value + other
                value = value.reshape(count * W, C)
                row = low + offset
                x_ref[pl.ds(row * W, count * W)] = value.astype(jnp.bfloat16)
                put(a_ref, row, count, value)

    @pl.when(first)
    def _():
        load_arrival.wait()
        fill("first")

    @pl.when(decoder)
    def _():
        load_skip.wait()
        fill("decoder")

    @pl.when(jnp.logical_not(jnp.logical_or(first, decoder)))
    def _():
        fill("encoder")

    def inside(value, row, count, reach):
        if row >= reach and row + count <= reach + ROWS:
            return value
        line = row - reach + lax.broadcasted_iota(jnp.int32, value.shape, 0) // W
        outside = jnp.logical_or(
            jnp.logical_and(rank == 0, line < 0),
            jnp.logical_and(rank == RANKS - 1, line >= ROWS),
        )
        return jnp.where(outside, 0.0, value)

    for row, count in tiles(total - 2, 4):
        value = silu(conv(a_ref, row, count, kernel_ref, bias_ref, 0))
        put(b_ref, row, count, inside(value, row, count, 2))
    for row, count in tiles(total - 4, 4):
        value = silu(conv(b_ref, row, count, kernel_ref, bias_ref, 1))
        put(a_ref, row, count, inside(value, row, count, 1))
    for row, count in tiles(ROWS, 4):
        value = conv(a_ref, row, count, kernel_ref, bias_ref, 2)
        value = value + x_ref[pl.ds((row + HALO) * W, count * W)].astype(jnp.float32)
        out_ref[pl.ds(row, count)] = value.astype(jnp.bfloat16).reshape(count, W, C)


def section(tick, held, aux, incoming, order=()):
    total = ROWS + 2 * HALO
    vmem = pl.BlockSpec(memory_space=pltpu.VMEM)
    anywhere = pl.BlockSpec(memory_space=pl.ANY)
    return pl.pallas_call(
        functools.partial(section_kernel, tick, len(order)),
        out_shape=jax.ShapeDtypeStruct((ROWS, W, C), jnp.bfloat16),
        in_specs=[anywhere] * 2 + [vmem] * 7 + [anywhere] * len(order),
        out_specs=vmem,
        scratch_shapes=[
            pltpu.VMEM((ROWS, W, C), jnp.bfloat16),
            pltpu.VMEM((total * W, C), jnp.bfloat16),
            pltpu.VMEM((total * W, 3 * C), jnp.bfloat16),
            pltpu.VMEM(((total - 2) * W, 3 * C), jnp.bfloat16),
            pltpu.SemaphoreType.DMA,
        ],
        compiler_params=pltpu.CompilerParams(vmem_limit_bytes=VMEM_LIMIT),
        cost_estimate=pl.CostEstimate(flops=0, bytes_accessed=0, transcendentals=0),
        name=f"section{tick}",
    )(*held, *aux, *incoming, *order)


def warm_kernel(skips_ref, arrivals_ref, kernel_ref, bias_ref, out_ref):
    out_ref[...] = jnp.zeros_like(out_ref) + bias_ref[0:1, 0:128]


def warm(held):
    vmem = pl.BlockSpec(memory_space=pltpu.VMEM)
    anywhere = pl.BlockSpec(memory_space=pl.ANY)
    return pl.pallas_call(
        warm_kernel,
        out_shape=jax.ShapeDtypeStruct((8, 128), jnp.float32),
        in_specs=[anywhere] * 2 + [vmem] * 2,
        out_specs=vmem,
        compiler_params=pltpu.CompilerParams(vmem_limit_bytes=VMEM_LIMIT),
        cost_estimate=pl.CostEstimate(flops=0, bytes_accessed=0, transcendentals=0),
        name="warm",
    )(*held)


def move(x, pairs):
    return lax.ppermute(x, AXES, pairs)


def links(step, sources, by=0):
    return [
        (s * RANKS + r, step(s) * RANKS + r + by)
        for s in sources
        for r in range(RANKS)
        if 0 <= r + by < RANKS
    ]


def following(s):
    return (s + 1) % SECTIONS


def same(s):
    return s


def mirror(s):
    return SECTIONS - 1 - s


HALF = SECTIONS // 2
DECODERS = range(HALF, SECTIONS)


def on_device(held_maps, held_skips, arrivals, kernels, biases):
    last = lax.axis_index("segment") == SECTIONS - 1
    held = (held_skips, arrivals, kernels[0], biases[0])

    def relay(tick, previous):
        low = jnp.where(last, arrivals[tick, ROWS - HALO :], previous[ROWS - HALO :])
        high = jnp.where(last, arrivals[tick, :HALO], previous[:HALO])
        return (
            move(previous, links(following, range(SECTIONS - 1))),
            move(low, links(following, range(SECTIONS), 1)),
            move(high, links(following, range(SECTIONS), -1)),
        )

    def stashed(made):
        return move(made, links(mirror, range(HALF)))

    aux = (
        move(held_skips[:, 0, ROWS - HALO :], links(same, DECODERS, 1)),
        move(held_skips[:, 0, :HALO], links(same, DECODERS, -1)),
    )
    map0 = section(0, held, aux, relay(0, held_maps[0]), (warm(held),))
    stash0 = stashed(map0)
    map1 = section(1, held, aux, relay(1, map0))
    stash1 = stashed(map1)
    map2 = section(2, held, aux, relay(2, map1), (stash0,))
    stash2 = stashed(map2)

    maps = jnp.stack([map0, map1, map2])
    stash = lax.dynamic_update_index_in_dim(
        jnp.stack([stash0, stash1, stash1]), stash2, TICKS - 1, 0
    )
    return maps[:, None], stash[:, None]


def solution(mesh):
    placed = (
        P("segment", "rows", None, None),
        P(None, "segment", "rows", None, None),
        P(None, "rows", None, None),
        P("segment", None, None, None, None),
        P("segment", None, None),
    )
    out = P(None, "segment", "rows", None, None)
    return jax.shard_map(
        on_device, mesh=mesh, in_specs=placed, out_specs=(out, out), check_vma=False
    )
```

```python
import functools

import jax
import jax.numpy as jnp
from jax import lax
from jax.experimental import pallas as pl
from jax.experimental.pallas import tpu as pltpu
from jax.sharding import PartitionSpec as P

TICKS = 3
SECTIONS = 16
RANKS = 8
HALO = 3
ROWS = 16
W = 64
C = 256
AXES = ("segment", "rows")
COST = 1
VMEM_LIMIT = 26 * 2**20


def tiles(total, size):
    return [(start, min(size, total - start)) for start in range(0, total, size)]


def put(dst, row, count, value):
    column = lax.broadcasted_iota(jnp.int32, value.shape, 0) % W
    left = jnp.where(column == 0, 0.0, pltpu.roll(value, 1, 0))
    right = jnp.where(column == W - 1, 0.0, pltpu.roll(value, value.shape[0] - 1, 0))
    rows = pl.ds(row * W, count * W)
    dst[rows, 0:C] = left.astype(jnp.bfloat16)
    dst[rows, C : 2 * C] = value.astype(jnp.bfloat16)
    dst[rows, 2 * C : 3 * C] = right.astype(jnp.bfloat16)


def conv(src, row, count, weights, bias_ref, layer):
    lhs = jnp.concatenate(
        [src[pl.ds((row + d) * W, count * W), :] for d in range(3)], axis=1
    )
    return (
        jnp.dot(lhs, weights[layer].reshape(9 * C, C), preferred_element_type=jnp.float32)
        + bias_ref[layer : layer + 1]
    )


def silu(v):
    return v * (0.5 * jnp.tanh(0.5 * v) + 0.5)


def section_kernel(
    tick, n_order,
    aux_ref, kernel_ref, bias_ref, aux_up_ref, aux_down_ref,
    main_ref, up_ref, down_ref, *rest,
):
    out_ref, x_ref, a_ref, b_ref = rest[n_order:]
    segment, rank = lax.axis_index("segment"), lax.axis_index("rows")
    total = ROWS + 2 * HALO
    first = segment == 0
    decoder = segment >= SECTIONS // 2

    def fill(role):
        pieces = ((0, HALO, up_ref, aux_up_ref), (HALO + ROWS, HALO, down_ref, aux_down_ref),
                  (HALO, ROWS, main_ref, None))
        for low, length, source, aux in pieces:
            if aux is None and role == "first":
                source = aux_ref
            for offset, count in tiles(length, 2):
                rows = pl.ds(offset, count)
                value = source[rows].astype(jnp.float32)
                if role == "decoder":
                    if aux is None:
                        other = aux_ref[rows]
                    else:
                        other = aux[tick, rows]
                    other = other.astype(jnp.float32)
                    if tick >= 1:
                        other = jnp.where(segment == SECTIONS // 2, value, other)
                    value = value + other
                value = value.reshape(count * W, C)
                row = low + offset
                x_ref[pl.ds(row * W, count * W)] = value.astype(jnp.bfloat16)
                put(a_ref, row, count, value)

    @pl.when(first)
    def _():
        fill("first")

    @pl.when(decoder)
    def _():
        fill("decoder")

    @pl.when(jnp.logical_not(jnp.logical_or(first, decoder)))
    def _():
        fill("encoder")

    def inside(value, row, count, reach):
        if row >= reach and row + count <= reach + ROWS:
            return value
        line = row - reach + lax.broadcasted_iota(jnp.int32, value.shape, 0) // W
        outside = jnp.logical_or(
            jnp.logical_and(rank == 0, line < 0),
            jnp.logical_and(rank == RANKS - 1, line >= ROWS),
        )
        return jnp.where(outside, 0.0, value)

    for row, count in tiles(total - 2, 4):
        value = silu(conv(a_ref, row, count, kernel_ref, bias_ref, 0))
        put(b_ref, row, count, inside(value, row, count, 2))
    for row, count in tiles(total - 4, 4):
        value = silu(conv(b_ref, row, count, kernel_ref, bias_ref, 1))
        put(a_ref, row, count, inside(value, row, count, 1))
    for row, count in tiles(ROWS, 4):
        value = conv(a_ref, row, count, kernel_ref, bias_ref, 2)
        value = value + x_ref[pl.ds((row + HALO) * W, count * W)].astype(jnp.float32)
        out_ref[pl.ds(row, count)] = value.astype(jnp.bfloat16).reshape(count, W, C)


def section(tick, held, aux, incoming, order=()):
    total = ROWS + 2 * HALO
    vmem = pl.BlockSpec(memory_space=pltpu.VMEM)
    anywhere = pl.BlockSpec(memory_space=pl.ANY)
    return pl.pallas_call(
        functools.partial(section_kernel, tick, len(order)),
        out_shape=jax.ShapeDtypeStruct((ROWS, W, C), jnp.bfloat16),
        in_specs=[vmem] * 8 + [anywhere] * len(order),
        out_specs=vmem,
        scratch_shapes=[
            pltpu.VMEM((total * W, C), jnp.bfloat16),
            pltpu.VMEM((total * W, 3 * C), jnp.bfloat16),
            pltpu.VMEM(((total - 2) * W, 3 * C), jnp.bfloat16),
        ],
        compiler_params=pltpu.CompilerParams(vmem_limit_bytes=VMEM_LIMIT),
        cost_estimate=pl.CostEstimate(
            flops=COST * 54 * W * 9 * C * C * 2, bytes_accessed=COST * 4 * 2**20, transcendentals=0
        ),
        name=f"section{tick}",
    )(*held, *aux, *incoming, *order)


def warm_kernel(kernel_ref, bias_ref, out_ref):
    out_ref[...] = jnp.zeros_like(out_ref) + bias_ref[0:1, 0:128]


def warm(held):
    vmem = pl.BlockSpec(memory_space=pltpu.VMEM)
    anywhere = pl.BlockSpec(memory_space=pl.ANY)
    return pl.pallas_call(
        warm_kernel,
        out_shape=jax.ShapeDtypeStruct((8, 128), jnp.float32),
        in_specs=[vmem] * 2,
        out_specs=vmem,
        compiler_params=pltpu.CompilerParams(vmem_limit_bytes=VMEM_LIMIT),
        cost_estimate=pl.CostEstimate(flops=0, bytes_accessed=0, transcendentals=0),
        name="warm",
    )(*held)


def move(x, pairs):
    return lax.ppermute(x, AXES, pairs)


def links(step, sources, by=0):
    return [
        (s * RANKS + r, step(s) * RANKS + r + by)
        for s in sources
        for r in range(RANKS)
        if 0 <= r + by < RANKS
    ]


def following(s):
    return (s + 1) % SECTIONS


def same(s):
    return s


def mirror(s):
    return SECTIONS - 1 - s


HALF = SECTIONS // 2
DECODERS = range(HALF, SECTIONS)


def on_device(held_maps, held_skips, arrivals, kernels, biases):
    segment = lax.axis_index("segment")
    last = segment == SECTIONS - 1
    held = (kernels[0], biases[0])

    def relay(tick, previous):
        low = jnp.where(last, arrivals[tick, ROWS - HALO :], previous[ROWS - HALO :])
        high = jnp.where(last, arrivals[tick, :HALO], previous[:HALO])
        return (
            move(previous, links(following, range(SECTIONS - 1))),
            move(low, links(following, range(SECTIONS), 1)),
            move(high, links(following, range(SECTIONS), -1)),
        )

    def joined(tick):
        return jnp.where(segment == 0, arrivals[tick], held_skips[tick, 0])

    def direct(made, sections):
        return move(made, links(mirror, sections))

    def forwarded(received):
        return move(
            received,
            [((s + 1) * RANKS + r, mirror(s) * RANKS + r) for s in (1, 3, 5) for r in range(RANKS)],
        )

    def mirrored(main, from_odd, from_even):
        kept = jnp.where(segment == HALF, main, from_odd)
        return jnp.where(lax.rem(segment, 2) == 0, kept, from_even)

    aux = (
        move(held_skips[:, 0, ROWS - HALO :], links(same, DECODERS, 1)),
        move(held_skips[:, 0, :HALO], links(same, DECODERS, -1)),
    )
    map0 = section(0, (joined(0), *held), aux, relay(0, held_maps[0]), (warm(held),))
    moved1 = relay(1, map0)
    even0 = direct(map0, range(0, HALF, 2))
    odd0 = forwarded(moved1[0])
    map1 = section(1, (joined(1), *held), aux, moved1)
    moved2 = relay(2, map1)
    even1 = direct(map1, range(0, HALF, 2))
    odd1 = forwarded(moved2[0])
    map2 = section(2, (joined(2), *held), aux, moved2, (even0, odd0))
    stash0 = mirrored(moved1[0], odd0, even0)
    stash1 = mirrored(moved2[0], odd1, even1)
    stash2 = direct(map2, range(HALF))

    maps = jnp.stack([map0, map1, map2])
    stash = lax.dynamic_update_index_in_dim(
        jnp.stack([stash0, stash1, stash1]), stash2, TICKS - 1, 0
    )
    return maps[:, None], stash[:, None]


def solution(mesh):
    placed = (
        P("segment", "rows", None, None),
        P(None, "segment", "rows", None, None),
        P(None, "rows", None, None),
        P("segment", None, None, None, None),
        P("segment", None, None),
    )
    out = P(None, "segment", "rows", None, None)
    return jax.shard_map(
        on_device, mesh=mesh, in_specs=placed, out_specs=(out, out), check_vma=False
    )
```

```python
import functools

import jax
import jax.numpy as jnp
from jax import lax
from jax.experimental import pallas as pl
from jax.experimental.pallas import tpu as pltpu
from jax.sharding import PartitionSpec as P

TICKS = 3
SECTIONS = 16
RANKS = 8
HALO = 3
ROWS = 16
W = 64
C = 256
AXES = ("segment", "rows")
COST = 1
VMEM_LIMIT = 26 * 2**20


def tiles(total, size):
    return [(start, min(size, total - start)) for start in range(0, total, size)]


def put(dst, row, count, value):
    column = lax.broadcasted_iota(jnp.int32, value.shape, 0) % W
    left = jnp.where(column == 0, 0.0, pltpu.roll(value, 1, 0))
    right = jnp.where(column == W - 1, 0.0, pltpu.roll(value, value.shape[0] - 1, 0))
    rows = pl.ds(row * W, count * W)
    dst[rows, 0:C] = left.astype(jnp.bfloat16)
    dst[rows, C : 2 * C] = value.astype(jnp.bfloat16)
    dst[rows, 2 * C : 3 * C] = right.astype(jnp.bfloat16)


def conv(src, row, count, weights, bias_ref, layer):
    lhs = jnp.concatenate(
        [src[pl.ds((row + d) * W, count * W), :] for d in range(3)], axis=1
    )
    return (
        jnp.dot(lhs, weights[layer].reshape(9 * C, C), preferred_element_type=jnp.float32)
        + bias_ref[layer : layer + 1]
    )


def silu(v):
    return v * (0.5 * jnp.tanh(0.5 * v) + 0.5)


def section_kernel(
    tick, n_order,
    aux_ref, kernel_ref, bias_ref, aux_up_ref, aux_down_ref,
    main_ref, up_ref, down_ref, *rest,
):
    out_ref, x_ref, a_ref, b_ref = rest[n_order:]
    segment, rank = lax.axis_index("segment"), lax.axis_index("rows")
    total = ROWS + 2 * HALO
    first = segment == 0
    decoder = segment >= SECTIONS // 2

    def fill(role):
        pieces = ((0, HALO, up_ref, aux_up_ref), (HALO + ROWS, HALO, down_ref, aux_down_ref),
                  (HALO, ROWS, main_ref, None))
        for low, length, source, aux in pieces:
            if aux is None and role == "first":
                source = aux_ref
            for offset, count in tiles(length, 2):
                rows = pl.ds(offset, count)
                value = source[rows].astype(jnp.float32)
                if role == "decoder":
                    if aux is None:
                        other = aux_ref[rows]
                    else:
                        other = aux[tick, rows]
                    other = other.astype(jnp.float32)
                    if tick >= 1:
                        other = jnp.where(segment == SECTIONS // 2, value, other)
                    value = value + other
                value = value.reshape(count * W, C)
                row = low + offset
                x_ref[pl.ds(row * W, count * W)] = value.astype(jnp.bfloat16)
                put(a_ref, row, count, value)

    @pl.when(first)
    def _():
        fill("first")

    @pl.when(decoder)
    def _():
        fill("decoder")

    @pl.when(jnp.logical_not(jnp.logical_or(first, decoder)))
    def _():
        fill("encoder")

    def inside(value, row, count, reach):
        if row >= reach and row + count <= reach + ROWS:
            return value
        line = row - reach + lax.broadcasted_iota(jnp.int32, value.shape, 0) // W
        outside = jnp.logical_or(
            jnp.logical_and(rank == 0, line < 0),
            jnp.logical_and(rank == RANKS - 1, line >= ROWS),
        )
        return jnp.where(outside, 0.0, value)

    for row, count in tiles(total - 2, 4):
        value = silu(conv(a_ref, row, count, kernel_ref, bias_ref, 0))
        put(b_ref, row, count, inside(value, row, count, 2))
    for row, count in tiles(total - 4, 4):
        value = silu(conv(b_ref, row, count, kernel_ref, bias_ref, 1))
        put(a_ref, row, count, inside(value, row, count, 1))
    for row, count in tiles(ROWS, 4):
        value = conv(a_ref, row, count, kernel_ref, bias_ref, 2)
        value = value + x_ref[pl.ds((row + HALO) * W, count * W)].astype(jnp.float32)
        out_ref[pl.ds(row, count)] = value.astype(jnp.bfloat16).reshape(count, W, C)


def section(tick, held, aux, incoming, order=()):
    total = ROWS + 2 * HALO
    vmem = pl.BlockSpec(memory_space=pltpu.VMEM)
    anywhere = pl.BlockSpec(memory_space=pl.ANY)
    return pl.pallas_call(
        functools.partial(section_kernel, tick, len(order)),
        out_shape=jax.ShapeDtypeStruct((ROWS, W, C), jnp.bfloat16),
        in_specs=[vmem] * 8 + [anywhere] * len(order),
        out_specs=vmem,
        scratch_shapes=[
            pltpu.VMEM((total * W, C), jnp.bfloat16),
            pltpu.VMEM((total * W, 3 * C), jnp.bfloat16),
            pltpu.VMEM(((total - 2) * W, 3 * C), jnp.bfloat16),
        ],
        compiler_params=pltpu.CompilerParams(vmem_limit_bytes=VMEM_LIMIT),
        cost_estimate=pl.CostEstimate(
            flops=COST * 54 * W * 9 * C * C * 2, bytes_accessed=COST * 4 * 2**20, transcendentals=0
        ),
        name=f"section{tick}",
    )(*held, *aux, *incoming, *order)


def warm_kernel(kernel_ref, bias_ref, out_ref):
    out_ref[...] = jnp.zeros_like(out_ref) + bias_ref[0:1, 0:128]


def warm(held):
    vmem = pl.BlockSpec(memory_space=pltpu.VMEM)
    anywhere = pl.BlockSpec(memory_space=pl.ANY)
    return pl.pallas_call(
        warm_kernel,
        out_shape=jax.ShapeDtypeStruct((8, 128), jnp.float32),
        in_specs=[vmem] * 2,
        out_specs=vmem,
        compiler_params=pltpu.CompilerParams(vmem_limit_bytes=VMEM_LIMIT),
        cost_estimate=pl.CostEstimate(flops=0, bytes_accessed=0, transcendentals=0),
        name="warm",
    )(*held)


def move(x, pairs):
    return lax.ppermute(x, AXES, pairs)


def links(step, sources, by=0):
    return [
        (s * RANKS + r, step(s) * RANKS + r + by)
        for s in sources
        for r in range(RANKS)
        if 0 <= r + by < RANKS
    ]


def following(s):
    return (s + 1) % SECTIONS


def same(s):
    return s


def mirror(s):
    return SECTIONS - 1 - s


HALF = SECTIONS // 2
DECODERS = range(HALF, SECTIONS)


def on_device(held_maps, held_skips, arrivals, kernels, biases):
    segment = lax.axis_index("segment")
    last = segment == SECTIONS - 1
    held = (kernels[0], biases[0])

    def relay(tick, previous):
        low = jnp.where(last, arrivals[tick, ROWS - HALO :], previous[ROWS - HALO :])
        high = jnp.where(last, arrivals[tick, :HALO], previous[:HALO])
        return (
            move(previous, links(following, range(SECTIONS - 1))),
            move(low, links(following, range(SECTIONS), 1)),
            move(high, links(following, range(SECTIONS), -1)),
        )

    def joined(tick):
        return jnp.where(segment == 0, arrivals[tick], held_skips[tick, 0])

    def direct(made, sections):
        return move(made, links(mirror, sections))

    def forwarded(received):
        return move(
            received,
            [((s + 1) * RANKS + r, mirror(s) * RANKS + r) for s in (1, 3, 5, 7) for r in range(RANKS)],
        )

    def mirrored(from_odd, from_even):
        return jnp.where(lax.rem(segment, 2) == 0, from_odd, from_even)

    aux = (
        move(held_skips[:, 0, ROWS - HALO :], links(same, DECODERS, 1)),
        move(held_skips[:, 0, :HALO], links(same, DECODERS, -1)),
    )
    map0 = section(0, (joined(0), *held), aux, relay(0, held_maps[0]), (warm(held),))
    moved1 = relay(1, map0)
    even0 = direct(map0, range(0, HALF, 2))
    odd0 = forwarded(moved1[0])
    map1 = section(1, (joined(1), *held), aux, moved1)
    moved2 = relay(2, map1)
    even1 = direct(map1, range(0, HALF, 2))
    odd1 = forwarded(moved2[0])
    map2 = section(2, (joined(2), *held), aux, moved2, (even0, odd0))
    stash0 = mirrored(odd0, even0)
    stash1 = mirrored(odd1, even1)
    stash2 = direct(map2, range(HALF))

    maps = jnp.stack([map0, map1, map2])
    stash = lax.dynamic_update_index_in_dim(
        jnp.stack([stash0, stash1, stash1]), stash2, TICKS - 1, 0
    )
    return maps[:, None], stash[:, None]


def solution(mesh):
    placed = (
        P("segment", "rows", None, None),
        P(None, "segment", "rows", None, None),
        P(None, "rows", None, None),
        P("segment", None, None, None, None),
        P("segment", None, None),
    )
    out = P(None, "segment", "rows", None, None)
    return jax.shard_map(
        on_device, mesh=mesh, in_specs=placed, out_specs=(out, out), check_vma=False
    )
```
